256 devices in a mesh: row: 8 (over x, z_hi), col: 32 (over y, z_lo, core).
Axes of the slice: x: 4, y: 4, z: 8 (z_hi: 2, z_lo: 4; z = z_hi * 4 + z_lo), core: 2. Of those that a mesh axis runs over, the one named last changes fastest.
Arguments:
- counts: int32 [16384, 32768], P('row', 'col'), may hold values from 0 to 64, as said below
- row_marg: int32 [16384], P('row'), may hold values from 3000 to 299999
- col_marg: int32 [32768], P('col'), may hold values from 3000 to 299999
- log_total: float32 [1], replicated, may hold values from 20 to 22
- row_emb: float32 [16384, 256], P(('row', 'col')), may hold values from -1.5 to 1.5
- row_accum: float32 [16384], P(('row', 'col')), may hold values from 983.04 to 983040
- col_emb: float32 [32768, 256], P(('col', 'row')), may hold values from -1.5 to 1.5
- col_accum: float32 [32768], P(('col', 'row')), may hold values from 491.52 to 491520
Outputs:
- new_row_emb: float32 [16384, 256], P(('row', 'col'))
- new_row_accum: float32 [16384], P(('row', 'col'))
- new_col_emb: float32 [32768, 256], P(('col', 'row'))
- new_col_accum: float32 [32768], P(('col', 'row'))
The draws below stay inside these ranges and needn't reach their ends.
Inputs may be any that keep to these rules, and one draw needn't show every extreme that they name: About half of the counts are zero; the nonzero ones spread over a range of powers of two.
All inputs are finite; a program needn't handle non-finite values.
Results may differ from the reference program's by a relative error of at most 0.0059.
Values may be sent and summed in bfloat16 or wider, within the bound.
No kernel may reach another device: no remote copies, remote signals or barrier semaphores. Data moves between devices by JAX's collectives and lax.ppermute only.
A program may use at most 64 MiB of HBM per device.

```python
import math
import jax
import jax.numpy as jnp
from jax import lax

D = 256
R = 2048
NR = 16384
NC = 32768


def draw_counts(key, part):
    key = jax.random.fold_in(key, 7)
    key_one, key_two, key_three = jax.random.split(key, 3)
    present = jax.random.randint(key_one, (NR, NC), 0, 2)
    powers = jax.random.randint(key_two, (NR, NC), 0, 7)
    upper = jnp.left_shift(jnp.ones((NR, NC), jnp.int32), powers) + 1
    values = jax.random.randint(key_three, (NR, NC), 1, upper)
    return jnp.where(present == 1, values, 0).astype(jnp.int32)


def plant(entries, key, least, top_value):
    longest = entries.shape.index(max(entries.shape))
    spots = []
    for shift in (0, 1):
        where = [jax.random.randint(jax.random.fold_in(key, axis), (), 0, length) for axis, length in enumerate(entries.shape)]
        where[longest] = (where[longest] + shift) % entries.shape[longest]
        spots.append(tuple(where))
    return entries.at[spots[0]].set(least).at[spots[1]].set(top_value)


def shard_levels(rng, dims, shards, smallest, high):
    def one(position, blocks):
        steps = jax.random.uniform(jax.random.fold_in(jax.random.fold_in(rng, 6), position), (blocks,), jnp.float32, smallest / len(shards), high / len(shards))
        return jnp.repeat(jnp.exp(steps), dims[position] // blocks).reshape((-1,) + (1,) * (len(dims) - position - 1))

    factor_of = one(*shards[0])
    for cut in shards[1:]:
        factor_of = factor_of * one(*cut)
    return factor_of


def noise(stream_key, dims, spread, most, shards=(), kind=jnp.bfloat16):
    level = shard_levels(stream_key, dims, shards, -0.22, 0.18) if shards else 1.0
    drawn = jax.random.normal(stream_key, dims, jnp.float32) * spread * level
    return jnp.minimum(jnp.maximum(drawn, -most), most).astype(kind)


def setup_inputs(seed: int = 0) -> dict:
    seeds = jax.random.split(jax.random.key(seed), 9)
    return {
        "counts": draw_counts(jax.random.fold_in(seeds[8], 71), 0),
        "row_marg": plant(jax.random.randint(seeds[1], (NR,), 3000, 300000), jax.random.fold_in(seeds[1], 1), 3000, 299999).astype(jnp.int32),
        "col_marg": plant(jax.random.randint(seeds[2], (NC,), 3000, 300000), jax.random.fold_in(seeds[2], 1), 3000, 299999).astype(jnp.int32),
        "log_total": jnp.clip(jax.random.uniform(seeds[3], (1,), jnp.float32, 20.0, 22.0), 20.0, 22.0),
        "row_emb": noise(seeds[4], (NR, D), 0.25, 1.5, ((0, 256),), jnp.float32),
        "row_accum": jnp.clip(jnp.exp(math.log(983040.0) - 6.9077553 * jax.random.uniform(seeds[5], (NR,), jnp.float32) ** shard_levels(seeds[5], (NR,), ((0, 256),), -0.2, 0.2)), 983.04, 983040.0),
        "col_emb": noise(seeds[6], (NC, D), 0.25, 1.5, ((0, 256),), jnp.float32),
        "col_accum": jnp.clip(jnp.exp(math.log(491520.0) - 6.9077553 * jax.random.uniform(seeds[7], (NC,), jnp.float32) ** shard_levels(seeds[7], (NC,), ((0, 256),), -0.2, 0.2)), 491.52, 491520.0),
    }


learn_rate = 0.5

def block_slopes(counts, row_vecs, col_vecs, row_marg, col_marg, log_total):
    scores = jnp.dot(row_vecs, col_vecs.T, preferred_element_type=jnp.float32)
    values = counts.astype(jnp.float32)
    shift = log_total[0] - jnp.log(row_marg.astype(jnp.float32))[:, None] - jnp.log(col_marg.astype(jnp.float32))[None, :]
    present = counts > 0
    target = jnp.log(jnp.where(present, values, 1.0)) + shift
    weight = 0.1 + 0.25 * jnp.sqrt(values)
    slopes = jnp.where(present, weight * (scores - target), jax.nn.sigmoid(scores - shift))
    return slopes.astype(jnp.bfloat16)

def adagrad(embed, accum, grad):
    accum_new = accum + lax.optimization_barrier(jnp.mean(grad * grad, axis=1))
    return (embed - learn_rate * grad / jnp.sqrt(accum_new)[:, None], accum_new)

def reference(counts, row_marg, col_marg, log_total, row_emb, row_accum, col_emb, col_accum):
    row_vecs = row_emb.astype(jnp.bfloat16)
    col_vecs = col_emb.astype(jnp.bfloat16)
    blocks = NR // R

    def one_block(carry, index):
        start = (index * R).astype(jnp.int32)
        rows_here = lax.dynamic_slice_in_dim(row_vecs, start, R, 0)
        counts_here = lax.dynamic_slice_in_dim(counts, start, R, 0)
        marg_here = lax.dynamic_slice_in_dim(row_marg, start, R, 0)
        slopes = block_slopes(counts_here, rows_here, col_vecs, marg_here, col_marg, log_total)
        row_part = jnp.dot(slopes, col_vecs, preferred_element_type=jnp.float32)
        col_part = lax.dot_general(slopes, rows_here, (((0,), (0,)), ((), ())), preferred_element_type=jnp.float32)
        return (carry + col_part, row_part)
    col_grad, row_parts = lax.scan(one_block, jnp.zeros((NC, D), jnp.float32), jnp.arange(blocks, dtype=jnp.int32))
    row_grad = row_parts.reshape(NR, D)
    new_row_emb, new_row_accum = adagrad(row_emb, row_accum, row_grad)
    new_col_emb, new_col_accum = adagrad(col_emb, col_accum, col_grad)
    return (new_row_emb, new_row_accum, new_col_emb, new_col_accum)
```

```python
import functools
import jax
import jax.numpy as jnp
from jax import lax
from jax.experimental import pallas as pl
from jax.experimental.pallas import tpu as pltpu
from jax.sharding import PartitionSpec as P

learn_rate = 0.5
LN2 = 0.6931471805599453
D = 256
VM = pl.BlockSpec(memory_space=pltpu.VMEM)


def main_kernel(strip, log_total, c0, c1, c2, c3, row_marg, col_marg,
                r0, r1, r2, r3, r4, r5, r6, r7, k0, k1, k2, k3,
                row_own, row_other, col_own, col_1, col_2, col_3,
                rows, cols, row_log, row_half, col_half, col_acc):
    step = pl.program_id(0)

    @pl.when(step == 0)
    def _():
        for i, piece in enumerate((r0, r1, r2, r3, r4, r5, r6, r7)):
            rows[i] = piece[...]
        for i, piece in enumerate((k0, k1, k2, k3)):
            for j in range(2):
                at = pl.multiple_of(strip[32 + 2 * i + j] * 128, 128)
                cols[pl.ds(at, 128), :] = piece[j * 128:(j + 1) * 128, :]
        row_log[...] = jnp.zeros_like(row_log)
        for i in range(32):
            row_log[i:i + 1, 0:64] = jnp.log(row_marg[pl.ds(strip[i], 1), :].astype(jnp.float32))
        turned = 0.5 * row_log[...].T
        for i in range(32):
            row_half[i // 4, (i % 4) * 64:(i % 4) * 64 + 64, :] = jnp.broadcast_to(turned[0:64, i:i + 1], (64, 128))
        col_half[...] = 0.5 * (jnp.log(col_marg[...].astype(jnp.float32)) - log_total[0])
        col_acc[...] = jnp.zeros_like(col_acc)

    r = rows[step]
    half = r * jnp.bfloat16(0.5)
    shift_r = row_half[step]
    shift_r = jnp.concatenate([shift_r, shift_r], axis=1)
    total = None
    for j in range(4):
        at = slice(j * 256, (j + 1) * 256)
        c = cols[at, :]
        s = lax.dot_general(half, c, (((1,), (1,)), ((), ())), preferred_element_type=jnp.float32)
        x = s + shift_r + col_half[:, at]
        n = jnp.concatenate([ref[:, at] for ref in (c0, c1, c2, c3)], axis=0).astype(jnp.float32)
        present = n > 0.0
        n = jnp.maximum(n, 1.0)
        weight = 0.2 + (0.5 * n) * lax.rsqrt(n)
        far = weight * (x - 0.5 * jnp.log(n))
        near = 0.5 * jnp.tanh(x) + 0.5
        slopes = jnp.where(present, far, near).astype(jnp.bfloat16)
        part = jnp.dot(slopes, c, preferred_element_type=jnp.float32)
        total = part if total is None else total + part
        col_acc[at, :] += lax.dot_general(slopes, r, (((0,), (0,)), ((), ())), preferred_element_type=jnp.float32)

    @pl.when(step < 4)
    def _():
        row_own[...] = total

    @pl.when(step >= 4)
    def _():
        row_other[...] = total.astype(jnp.bfloat16)

    @pl.when(step == 7)
    def _():
        for i, out in enumerate((col_own, col_1, col_2, col_3)):
            for j in range(2):
                at = pl.multiple_of(strip[32 + 2 * i + j] * 128, 128)
                out[j * 128:(j + 1) * 128, :] = col_acc[pl.ds(at, 128), :].astype(out.dtype)


def main_call(strip, log_total, counts, row_marg, col_marg, rows, cols):
    whole = lambda shape: pl.BlockSpec(shape, lambda i, s: (0,) * len(shape))
    f32, bf16 = jnp.float32, jnp.bfloat16
    spec = pltpu.PrefetchScalarGridSpec(
        num_scalar_prefetch=1,
        grid=(8,),
        in_specs=[pl.BlockSpec(memory_space=pltpu.SMEM)]
        + [pl.BlockSpec((64, 1024), functools.partial(lambda k, i, s: (s[4 * i + k], 0), k)) for k in range(4)]
        + [whole((32, 64)), whole((1, 1024))]
        + [whole((256, D))] * 12,
        out_specs=[
            pl.BlockSpec((256, D), lambda i, s: (jnp.minimum(i, 3), 0)),
            pl.BlockSpec((256, D), lambda i, s: (jnp.maximum(i - 4, 0), 0)),
        ] + [whole((256, D))] * 4,
        scratch_shapes=[
            pltpu.VMEM((8, 256, D), bf16),
            pltpu.VMEM((1024, D), bf16),
            pltpu.VMEM((128, 128), f32),
            pltpu.VMEM((8, 256, 128), f32),
            pltpu.VMEM((1, 1024), f32),
            pltpu.VMEM((1024, D), f32),
        ],
    )
    piece = lambda n, t: jax.ShapeDtypeStruct((n, D), t)
    return pl.pallas_call(
        main_kernel,
        grid_spec=spec,
        out_shape=[piece(1024, f32), piece(1024, bf16), piece(256, f32)] + [piece(256, bf16)] * 3,
        compiler_params=pltpu.CompilerParams(vmem_limit_bytes=40 << 20, dimension_semantics=("arbitrary",)),
        cost_estimate=pl.CostEstimate(flops=3 * 2 * 2048 * 1024 * 256, bytes_accessed=12 << 20, transcendentals=6 << 20),
    )(strip, log_total, counts, counts, counts, counts, row_marg, col_marg, *rows, *cols)


def fold_kernel(n, *refs):
    own, got, outs = refs[0], refs[1:1 + n], refs[1 + n:]
    rows = outs[0].shape[0]
    for i, out in enumerate(outs):
        at = slice(i * rows, (i + 1) * rows)
        total = own[at, :]
        for ref in got:
            total = total + ref[at, :].astype(jnp.float32)
        out[...] = total.astype(out.dtype)


def fold(own, got, parts):
    rows = own.shape[0] // parts
    return pl.pallas_call(
        functools.partial(fold_kernel, len(got)),
        in_specs=[VM] * (1 + len(got)),
        out_specs=[VM] * parts,
        out_shape=[jax.ShapeDtypeStruct((rows, D), jnp.float32)]
        + [jax.ShapeDtypeStruct((rows, D), jnp.bfloat16)] * (parts - 1),
        compiler_params=pltpu.CompilerParams(vmem_limit_bytes=16 << 20),
    )(own, *got)


def adagrad_kernel(n, *refs):
    own, got, embed, accum, embed_out, accum_out = refs[0], refs[1:1 + n], *refs[1 + n:]
    rows = own.shape[0]
    grad = own[...]
    for ref in got:
        grad = grad + ref[...].astype(jnp.float32)
    line = jnp.concatenate([accum[...]] * (128 // rows), axis=1)
    column = jnp.broadcast_to(line, (128, 128)).T[0:rows, 0:1]
    new = column + jnp.mean(grad * grad, axis=1, keepdims=True)
    embed_out[...] = embed[...] - learn_rate * grad / jnp.sqrt(new)
    tall = jnp.concatenate([jnp.broadcast_to(new, (rows, 128))] * (128 // rows), axis=0)
    accum_out[...] = tall.T[0:1, 0:rows]


def adagrad(own, got, embed, accum):
    rows = own.shape[0]
    new_embed, new_accum = pl.pallas_call(
        functools.partial(adagrad_kernel, len(got)),
        in_specs=[VM] * (3 + len(got)),
        out_specs=[VM] * 2,
        out_shape=[jax.ShapeDtypeStruct((rows, D), jnp.float32), jax.ShapeDtypeStruct((1, rows), jnp.float32)],
        compiler_params=pltpu.CompilerParams(vmem_limit_bytes=16 << 20),
    )(own, *got, embed, accum.reshape(1, rows))
    return new_embed, new_accum.reshape(rows)


def swap(x, axis, size, flip):
    return lax.ppermute(x, axis, [(i, i ^ flip) for i in range(size)])


def per_device(counts, row_marg, col_marg, log_total, row_emb, row_accum, col_emb, col_accum):
    col_swap = lambda x, flip: swap(x, "col", 32, flip)
    row_swap = lambda x, flip: swap(x, "row", 8, flip)
    me_c, me_r = lax.axis_index("col"), lax.axis_index("row")
    flips = [8 * ky + 2 * kz + kc for kc in range(2) for ky in range(4) for kz in range(4)]
    strip = jnp.concatenate([
        me_c ^ jnp.array(flips, jnp.int32),
        me_r ^ jnp.arange(8, dtype=jnp.int32),
    ])

    col_mine = col_emb.astype(jnp.bfloat16)
    col_pair = jnp.concatenate([col_mine, row_swap(col_mine, 1)], axis=0)
    row_mine = row_emb.astype(jnp.bfloat16)
    row_four = jnp.concatenate([row_mine] + [col_swap(row_mine, 2 * k) for k in (1, 2, 3)], axis=0)
    cols = [col_pair] + [row_swap(col_pair, 2 * k) for k in (1, 2, 3)]
    rows = [row_four] + [col_swap(row_four, 8 * k) for k in (1, 2, 3)]
    rows = rows + [col_swap(x, 1) for x in rows]

    row_own, row_other, col_own, *col_send = main_call(
        strip, log_total, counts, row_marg.reshape(32, 64), col_marg.reshape(1, 1024), rows, cols)

    row_got = col_swap(row_other, 1)
    col_got = [row_swap(x, 2 * k) for k, x in zip((1, 2, 3), col_send)]
    row_own, *row_send = fold(row_own, [row_got], 4)
    row_got = [col_swap(x, 8 * k) for k, x in zip((1, 2, 3), row_send)]
    col_own, col_last = fold(col_own, col_got, 2)
    col_got = [row_swap(col_last, 1)]
    row_own, *row_send = fold(row_own, row_got, 4)
    row_got = [col_swap(x, 2 * k) for k, x in zip((1, 2, 3), row_send)]
    new_col_emb, new_col_accum = adagrad(col_own, col_got, col_emb, col_accum)
    new_row_emb, new_row_accum = adagrad(row_own, row_got, row_emb, row_accum)
    return (new_row_emb, new_row_accum, new_col_emb, new_col_accum)


def solution(mesh):
    return jax.shard_map(
        per_device,
        mesh=mesh,
        in_specs=(
            P("row", "col"),
            P("row"),
            P("col"),
            P(),
            P(("row", "col"), None),
            P(("row", "col")),
            P(("col", "row"), None),
            P(("col", "row")),
        ),
        out_specs=(
            P(("row", "col"), None),
            P(("row", "col")),
            P(("col", "row"), None),
            P(("col", "row")),
        ),
        check_vma=False,
    )
```

```python
import functools
import jax
import jax.numpy as jnp
from jax import lax
from jax.experimental import pallas as pl
from jax.experimental.pallas import tpu as pltpu
from jax.sharding import PartitionSpec as P

learn_rate = 0.5
D = 256
f32, bf16 = jnp.float32, jnp.bfloat16
VM = pl.BlockSpec(memory_space=pltpu.VMEM)
SM = pl.BlockSpec(memory_space=pltpu.SMEM)


def call(kernel, outs, ins, in_specs=None, scratch=(), limit=8, cost=None):
    return pl.pallas_call(
        kernel,
        in_specs=in_specs or [VM] * len(ins),
        out_specs=[VM] * len(outs),
        out_shape=[jax.ShapeDtypeStruct(s, t) for s, t in outs],
        scratch_shapes=list(scratch),
        compiler_params=pltpu.CompilerParams(vmem_limit_bytes=limit << 20),
        cost_estimate=cost,
    )(*ins)


def by_core(zero, one):
    core = lax.axis_index("col") % 2
    pl.when(core == 0)(zero)
    pl.when(core == 1)(one)


def first_kernel(row_emb, col_emb, row, col, out, row_buf, col_buf, sem):
    copies = [
        pltpu.make_async_copy(row_emb, row_buf, sem.at[0]),
        pltpu.make_async_copy(col_emb, col_buf, sem.at[1]),
    ]
    for copy in copies:
        copy.start()
    for copy in copies:
        copy.wait()
    row[...] = row_buf[...].astype(bf16)
    col[...] = col_buf[...].astype(bf16)

    def zero():
        out[...] = col_buf[...].astype(bf16)

    def one():
        out[0:64, :] = row_buf[...].astype(bf16)
        out[64:128, :] = jnp.zeros((64, D), bf16)

    by_core(zero, one)


def second_kernel(row, col, got, a, b):
    def zero():
        for out in (a, b):
            out[0:64, :] = row[...]
            out[64:128, :] = got[0:64, :]

    def one():
        a[...] = got[...]
        b[...] = col[...]

    by_core(zero, one)


def third_kernel(token, a, b, g1, g2, g3, out):
    def put(*parts):
        for i, part in enumerate(parts):
            out[i * 128:(i + 1) * 128, :] = part[...]

    by_core(lambda: put(a, g1, g2, g3), lambda: put(a, b, g1, g2))


def tie_kernel(x, *refs):
    refs[-1][...] = x[...]


def tie(x, *after):
    return call(tie_kernel, [(x.shape, x.dtype)], (x, *after))[0]


def slope_parts_kernel(half, after, log_total, row_marg, col_marg, counts, *refs):
    weight, base, token, buf, row_buf, col_buf, sem, row_log, row_half, col_half = refs[after:]
    token[...] = jnp.zeros_like(token)
    me = lax.axis_index("row"), lax.axis_index("col")
    core = me[1] % 2
    group = lambda i: (me[1] // 2) ^ (i + 8 * half)

    def copy(i):
        at = pl.multiple_of(group(i) * 128, 128)
        return pltpu.make_async_copy(counts.at[pl.ds(at, 128), :], buf.at[i], sem.at[i])

    small = [
        pltpu.make_async_copy(row_marg, row_buf, sem.at[8]),
        pltpu.make_async_copy(col_marg, col_buf, sem.at[9]),
    ]
    for one in small:
        one.start()
    for i in range(8):
        copy(i).start()
    row_log[...] = jnp.zeros_like(row_log)
    for one in small:
        one.wait()
    for i in range(8):
        row_log[i:i + 1, :] = jnp.log(row_buf[pl.ds(group(i), 1), :].astype(f32))
    turned = 0.5 * row_log[...].T
    for i in range(8):
        row_half[i] = jnp.broadcast_to(turned[:, i:i + 1], (128, 128))
    col_half[...] = 0.5 * (jnp.log(col_buf[...].astype(f32)) - log_total[0])

    def body(i, carry):
        copy(i).wait()
        first = pl.ds(pl.multiple_of(i * 64 + core * 512, 64), 64)
        second = pl.ds(pl.multiple_of(i * 64 + (1 - core) * 512, 64), 64)
        shift = row_half[i]
        for j in range(8):
            strip = me[0] ^ j
            n = buf[i, :, pl.ds(pl.multiple_of(strip * 128, 128), 128)].astype(f32)
            present = n > 0.0
            n = jnp.maximum(n, 1.0)
            at = slice(j * 128, (j + 1) * 128)
            w = jnp.where(present, 0.2 + (0.5 * n) * lax.rsqrt(n), 0.0)
            b = (shift + col_half[pl.ds(strip, 1), :]) - 0.5 * jnp.log(n)
            weight[first, at] = w[0:64, :]
            weight[second, at] = w[64:128, :]
            base[first, at] = b[0:64, :]
            base[second, at] = b[64:128, :]
        return carry

    lax.fori_loop(0, 8, body, 0)


def slope_parts(half, log_total, row_marg, col_marg, counts, after=()):
    hbm = pl.BlockSpec(memory_space=pltpu.HBM)
    keep = lambda x: pltpu.with_memory_space_constraint(x, pltpu.HBM)
    return call(
        functools.partial(slope_parts_kernel, half, len(after)),
        [((1024, 1024), f32)] * 2 + [((8, 128), f32)],
        (log_total, keep(row_marg.reshape(16, 128)), keep(col_marg.reshape(8, 128)), keep(counts), *after),
        in_specs=[SM, hbm, hbm, hbm] + [VM] * len(after),
        scratch=[
            pltpu.VMEM((8, 128, 1024), jnp.int32),
            pltpu.VMEM((16, 128), jnp.int32),
            pltpu.VMEM((8, 128), jnp.int32),
            pltpu.SemaphoreType.DMA((10,)),
            pltpu.VMEM((128, 128), f32),
            pltpu.VMEM((8, 128, 128), f32),
            pltpu.VMEM((8, 128), f32),
        ],
        limit=8,
        cost=pl.CostEstimate(flops=0, bytes_accessed=10 << 20, transcendentals=2 << 20),
    )


def main_kernel(weight_a, base_a, weight_b, base_b, *refs):
    (mine, got, (row_own, row_other, col_own, col_1, col_2, col_3),
     (rows, cols, row_acc, col_acc)) = refs[0:4], refs[4:8], refs[8:14], refs[14:]

    def gather(row_parts, col_parts, core):
        for i, part in enumerate(row_parts):
            for j in range(4):
                for k in range(2):
                    at = j * 128 + (core ^ k) * 64
                    to = (i // 2) * 1024 + k * 512 + (i % 2) * 256 + j * 64
                    rows[to:to + 64, :] = part[at:at + 64, :]
        for i, part in enumerate(col_parts):
            for j in range(2):
                at = j * 256 + core * 128
                to = i * 256 + j * 128
                cols[to:to + 128, :] = part[at:at + 128, :]

    by_core(lambda: gather(mine, got, 0), lambda: gather(got, mine, 1))
    for j in range(4):
        at = slice(j * 256, (j + 1) * 256)
        c = cols[at, :]
        col = None
        for h, (weight, base) in enumerate(((weight_a, base_a), (weight_b, base_b))):
            here = slice(h * 1024, (h + 1) * 1024)
            r = rows[here, :]
            x = lax.dot_general(r * bf16(0.5), c, (((1,), (1,)), ((), ())), preferred_element_type=f32) + base[:, at]
            w = weight[:, at]
            slopes = jnp.where(w > 0.0, w * x, 0.5 * jnp.tanh(x) + 0.5).astype(bf16)
            part = jnp.dot(slopes, c, preferred_element_type=f32)
            row_acc[here, :] = part if j == 0 else row_acc[here, :] + part
            part = lax.dot_general(slopes, r, (((0,), (0,)), ((), ())), preferred_element_type=f32)
            col = part if col is None else col + part
        (col_own, col_1, col_2, col_3)[j][...] = col.astype(f32 if j == 0 else bf16)
    for h in range(2):
        to = slice(h * 512, (h + 1) * 512)
        row_own[to, :] = row_acc[h * 1024:h * 1024 + 512, :]
        row_other[to, :] = row_acc[h * 1024 + 512:(h + 1) * 1024, :].astype(bf16)


def fold_kernel(n, *refs):
    own, got, outs = refs[0], refs[1:1 + n], refs[1 + n:]
    at = 0
    for out in outs:
        rows = slice(at, at + out.shape[0])
        at += out.shape[0]
        total = own[rows, :]
        for ref in got:
            total = total + ref[rows, :].astype(f32)
        out[...] = total.astype(out.dtype)


def fold(own, got, *parts):
    outs = [((rows, D), bf16 if i else f32) for i, rows in enumerate(parts)]
    return call(functools.partial(fold_kernel, len(got)), outs, (own, *got))


def adagrad_part(grad, embed, accum, embed_out, accum_out):
    rows = embed.shape[0]
    line = jnp.concatenate([accum[...]] * (128 // rows), axis=1)
    column = jnp.broadcast_to(line, (128, 128)).T[0:rows, 0:1]
    new = column + jnp.mean(grad * grad, axis=1, keepdims=True)
    embed_out[...] = embed[...] - learn_rate * grad / jnp.sqrt(new)
    tall = jnp.concatenate([jnp.broadcast_to(new, (rows, 128))] * (128 // rows), axis=0)
    accum_out[...] = tall.T[0:1, 0:rows]


def adagrad_kernel(n, *refs):
    own, got, embed, accum, embed_out, accum_out = refs[0], refs[1:1 + n], *refs[1 + n:]
    grad = own[...]
    for ref in got:
        grad = grad + ref[...].astype(f32)
    adagrad_part(grad, embed, accum, embed_out, accum_out)


def adagrad(own, got, embed, accum):
    rows = own.shape[0]
    new_embed, new_accum = call(
        functools.partial(adagrad_kernel, len(got)),
        [((rows, D), f32), ((1, rows), f32)],
        (own, *got, embed, accum.reshape(1, rows)),
    )
    return new_embed, new_accum.reshape(rows)


def swap(x, axis, size, flip):
    return lax.ppermute(x, axis, [(i, i ^ flip) for i in range(size)])


def hop(x, zero, one):
    pairs = []
    for r in range(8):
        for c in range(32):
            if c % 2 == 0:
                pairs.append((r * 32 + c, r * 32 + (c ^ zero)))
            elif one:
                pairs.append((r * 32 + c, (r ^ one) * 32 + c))
    return lax.ppermute(x, ("row", "col"), pairs)


def per_device(counts, row_marg, col_marg, log_total, row_emb, row_accum, col_emb, col_accum):
    col_swap = lambda x, flip: swap(x, "col", 32, flip)
    row_swap = lambda x, flip: swap(x, "row", 8, flip)
    block = lambda n, t=bf16: ((n, D), t)
    hbm = pl.BlockSpec(memory_space=pltpu.HBM)

    keep = lambda x: pltpu.with_memory_space_constraint(x, pltpu.HBM)
    row, col, out = call(
        first_kernel, [block(64), block(128), block(128)], (keep(row_emb), keep(col_emb)), in_specs=[hbm, hbm],
        scratch=[pltpu.VMEM((64, D), f32), pltpu.VMEM((128, D), f32), pltpu.SemaphoreType.DMA((2,))],
    )
    margs = log_total, row_marg, col_marg, counts
    a, b = call(second_kernel, [block(128)] * 2, (row, col, col_swap(out, 1)))
    near = [hop(a, 2, 1), hop(b, 4, 1), hop(a, 6, 0)]
    weight_a, base_a, token = slope_parts(0, *margs, after=(a,))
    mine = list(call(third_kernel, [block(512)], (token, a, b, *near)))
    mine = mine + [hop(mine[0], 8 * k, 2 * k) for k in (1, 2, 3)]
    weight_b, base_b, token = slope_parts(1, *margs, after=(mine[0],))
    mine = mine[0:1] + [tie(x, token) for x in mine[1:]]
    got = [col_swap(x, 1) for x in mine]

    row_own, row_other, col_own, *col_send = call(
        main_kernel,
        [block(1024, f32), block(1024), block(256, f32)] + [block(256)] * 3,
        (weight_a, base_a, weight_b, base_b, *mine, *got),
        scratch=[pltpu.VMEM((2048, D), bf16), pltpu.VMEM((1024, D), bf16),
                 pltpu.VMEM((2048, D), f32), pltpu.VMEM((1024, D), f32)],
        limit=24,
        cost=pl.CostEstimate(flops=3 << 30, bytes_accessed=16 << 20, transcendentals=2 << 20),
    )

    row_got = col_swap(row_other, 1)
    col_got = [row_swap(x, 2 * k) for k, x in zip((1, 2, 3), col_send)]
    row_own, *row_send = fold(row_own, [row_got], 256, 256, 256, 256)
    row_got = [col_swap(x, 8 * k) for k, x in zip((1, 2, 3), row_send)]
    col_own, col_last = fold(col_own, col_got, 128, 128)
    col_got = [row_swap(col_last, 1)]
    row_own, *row_send = fold(row_own, row_got, 64, 64, 64, 64)
    row_got = [col_swap(x, 2 * k) for k, x in zip((1, 2, 3), row_send)]
    new_col_emb, new_col_accum = adagrad(col_own, col_got, col_emb, col_accum)
    new_row_emb, new_row_accum = adagrad(row_own, row_got, row_emb, row_accum)
    return (new_row_emb, new_row_accum, new_col_emb, new_col_accum)


def solution(mesh):
    return jax.shard_map(
        per_device,
        mesh=mesh,
        in_specs=(
            P("row", "col"),
            P("row"),
            P("col"),
            P(),
            P(("row", "col"), None),
            P(("row", "col")),
            P(("col", "row"), None),
            P(("col", "row")),
        ),
        out_specs=(
            P(("row", "col"), None),
            P(("row", "col")),
            P(("col", "row"), None),
            P(("col", "row")),
        ),
        check_vma=False,
    )
```

```python
import functools
import jax
import jax.numpy as jnp
from jax import lax
from jax.experimental import pallas as pl
from jax.experimental.pallas import tpu as pltpu
from jax.sharding import PartitionSpec as P

learn_rate = 0.5
D = 256
f32, bf16 = jnp.float32, jnp.bfloat16
VM = pl.BlockSpec(memory_space=pltpu.VMEM)
SM = pl.BlockSpec(memory_space=pltpu.SMEM)


def call(kernel, outs, ins, in_specs=None, scratch=(), limit=8, cost=None):
    return pl.pallas_call(
        kernel,
        in_specs=in_specs or [VM] * len(ins),
        out_specs=[VM] * len(outs),
        out_shape=[jax.ShapeDtypeStruct(s, t) for s, t in outs],
        scratch_shapes=list(scratch),
        compiler_params=pltpu.CompilerParams(vmem_limit_bytes=limit << 20),
        cost_estimate=cost,
    )(*ins)


def by_core(zero, one):
    core = lax.axis_index("col") % 2
    pl.when(core == 0)(zero)
    pl.when(core == 1)(one)


def first_kernel(row_emb, col_emb, row, col, out, row_buf, col_buf, sem):
    copies = [
        pltpu.make_async_copy(row_emb, row_buf, sem.at[0]),
        pltpu.make_async_copy(col_emb, col_buf, sem.at[1]),
    ]
    for copy in copies:
        copy.start()
    for copy in copies:
        copy.wait()
    row[...] = row_buf[...].astype(bf16)
    col[...] = col_buf[...].astype(bf16)

    def zero():
        out[...] = col_buf[...].astype(bf16)

    def one():
        out[0:64, :] = row_buf[...].astype(bf16)
        out[64:128, :] = jnp.zeros((64, D), bf16)

    by_core(zero, one)


def second_kernel(row, col, got, a, b):
    def zero():
        for out in (a, b):
            out[0:64, :] = row[...]
            out[64:128, :] = got[0:64, :]

    def one():
        a[...] = got[...]
        b[...] = col[...]

    by_core(zero, one)


def third_kernel(token, a, b, g1, g2, g3, out):
    def put(*parts):
        for i, part in enumerate(parts):
            out[i * 128:(i + 1) * 128, :] = part[...]

    by_core(lambda: put(a, g1, g2, g3), lambda: put(a, b, g1, g2))


def tie_kernel(x, *refs):
    refs[-1][...] = x[...]


def tie(x, *after):
    return call(tie_kernel, [(x.shape, x.dtype)], (x, *after))[0]


def slope_parts_kernel(half, after, log_total, row_marg, col_marg, counts, *refs):
    weight, base, token, buf, row_buf, col_buf, sem, row_log, row_half, col_half = refs[after:]
    token[...] = jnp.zeros_like(token)
    me = lax.axis_index("row"), lax.axis_index("col")
    core = me[1] % 2
    group = lambda i: (me[1] // 2) ^ (i + 8 * half)

    def copy(i):
        at = pl.multiple_of(group(i) * 128, 128)
        return pltpu.make_async_copy(counts.at[pl.ds(at, 128), :], buf.at[i], sem.at[i])

    small = [
        pltpu.make_async_copy(row_marg, row_buf, sem.at[8]),
        pltpu.make_async_copy(col_marg, col_buf, sem.at[9]),
    ]
    for one in small:
        one.start()
    for i in range(8):
        copy(i).start()
    row_log[...] = jnp.zeros_like(row_log)
    for one in small:
        one.wait()
    for i in range(8):
        row_log[i:i + 1, :] = jnp.log(row_buf[pl.ds(group(i), 1), :].astype(f32))
    turned = 0.5 * row_log[...].T
    for i in range(8):
        row_half[i] = jnp.broadcast_to(turned[:, i:i + 1], (128, 128))
    col_half[...] = 0.5 * (jnp.log(col_buf[...].astype(f32)) - log_total[0])

    def body(i, carry):
        copy(i).wait()
        first = pl.ds(pl.multiple_of(i * 64 + core * 512, 64), 64)
        second = pl.ds(pl.multiple_of(i * 64 + (1 - core) * 512, 64), 64)
        shift = row_half[i]
        for j in range(8):
            strip = me[0] ^ j
            n = buf[i, :, pl.ds(pl.multiple_of(strip * 128, 128), 128)].astype(f32)
            present = n > 0.0
            n = jnp.maximum(n, 1.0)
            at = slice(j * 128, (j + 1) * 128)
            w = jnp.where(present, 0.2 + (0.5 * n) * lax.rsqrt(n), 0.0)
            b = (shift + col_half[pl.ds(strip, 1), :]) - 0.5 * jnp.log(n)
            weight[first, at] = w[0:64, :]
            weight[second, at] = w[64:128, :]
            base[first, at] = b[0:64, :]
            base[second, at] = b[64:128, :]
        return carry

    lax.fori_loop(0, 8, body, 0)


def slope_parts(half, log_total, row_marg, col_marg, counts, after=()):
    hbm = pl.BlockSpec(memory_space=pltpu.HBM)
    keep = lambda x: pltpu.with_memory_space_constraint(x, pltpu.HBM)
    return call(
        functools.partial(slope_parts_kernel, half, len(after)),
        [((1024, 1024), f32)] * 2 + [((8, 128), f32)],
        (log_total, keep(row_marg.reshape(16, 128)), keep(col_marg.reshape(8, 128)), keep(counts), *after),
        in_specs=[SM, hbm, hbm, hbm] + [VM] * len(after),
        scratch=[
            pltpu.VMEM((8, 128, 1024), jnp.int32),
            pltpu.VMEM((16, 128), jnp.int32),
            pltpu.VMEM((8, 128), jnp.int32),
            pltpu.SemaphoreType.DMA((10,)),
            pltpu.VMEM((128, 128), f32),
            pltpu.VMEM((8, 128, 128), f32),
            pltpu.VMEM((8, 128), f32),
        ],
        limit=8,
        cost=pl.CostEstimate(flops=0, bytes_accessed=10 << 20, transcendentals=2 << 20),
    )


def main_kernel(weight_a, base_a, weight_b, base_b, *refs):
    (mine, got, (row_own, row_other, col_own, col_1, col_2, col_3),
     (rows, cols, row_acc, col_acc)) = refs[0:4], refs[4:8], refs[8:14], refs[14:]

    def gather(row_parts, col_parts, core):
        for i, part in zip((0,) + (2, 1, 3), row_parts):
            for j in range(4):
                for k in range(2):
                    at = j * 128 + (core ^ k) * 64
                    to = (i // 2) * 1024 + k * 512 + (i % 2) * 256 + j * 64
                    rows[to:to + 64, :] = part[at:at + 64, :]
        for i, part in zip((0,) + (2, 1, 3), col_parts):
            for j in range(2):
                at = j * 256 + core * 128
                to = i * 256 + j * 128
                cols[to:to + 128, :] = part[at:at + 128, :]

    by_core(lambda: gather(mine, got, 0), lambda: gather(got, mine, 1))
    for j in range(4):
        at = slice(j * 256, (j + 1) * 256)
        c = cols[at, :]
        col = None
        for h, (weight, base) in enumerate(((weight_a, base_a), (weight_b, base_b))):
            here = slice(h * 1024, (h + 1) * 1024)
            r = rows[here, :]
            x = lax.dot_general(r * bf16(0.5), c, (((1,), (1,)), ((), ())), preferred_element_type=f32) + base[:, at]
            w = weight[:, at]
            slopes = jnp.where(w > 0.0, w * x, 0.5 * jnp.tanh(x) + 0.5).astype(bf16)
            part = jnp.dot(slopes, c, preferred_element_type=f32)
            row_acc[here, :] = part if j == 0 else row_acc[here, :] + part
            part = lax.dot_general(slopes, r, (((0,), (0,)), ((), ())), preferred_element_type=f32)
            col = part if col is None else col + part
        (col_own, col_1, col_2, col_3)[j][...] = col.astype(f32 if j == 0 else bf16)
    for h in range(2):
        to = slice(h * 512, (h + 1) * 512)
        row_own[to, :] = row_acc[h * 1024:h * 1024 + 512, :]
        row_other[to, :] = row_acc[h * 1024 + 512:(h + 1) * 1024, :].astype(bf16)


def fold_kernel(n, *refs):
    own, got, outs = refs[0], refs[1:1 + n], refs[1 + n:]
    at = 0
    for out in outs:
        rows = slice(at, at + out.shape[0])
        at += out.shape[0]
        total = own[rows, :]
        for ref in got:
            total = total + ref[rows, :].astype(f32)
        out[...] = total.astype(out.dtype)


def fold(own, got, *parts):
    outs = [((rows, D), bf16 if i else f32) for i, rows in enumerate(parts)]
    return call(functools.partial(fold_kernel, len(got)), outs, (own, *got))


def adagrad_part(grad, embed, accum, embed_out, accum_out):
    rows = embed.shape[0]
    line = jnp.concatenate([accum[...]] * (128 // rows), axis=1)
    column = jnp.broadcast_to(line, (128, 128)).T[0:rows, 0:1]
    new = column + jnp.mean(grad * grad, axis=1, keepdims=True)
    embed_out[...] = embed[...] - learn_rate * grad / jnp.sqrt(new)
    tall = jnp.concatenate([jnp.broadcast_to(new, (rows, 128))] * (128 // rows), axis=0)
    accum_out[...] = tall.T[0:1, 0:rows]


def adagrad_kernel(n, *refs):
    own, got, embed, accum, embed_out, accum_out = refs[0], refs[1:1 + n], *refs[1 + n:]
    grad = own[...]
    for ref in got:
        grad = grad + ref[...].astype(f32)
    adagrad_part(grad, embed, accum, embed_out, accum_out)


def adagrad(own, got, embed, accum):
    rows = own.shape[0]
    new_embed, new_accum = call(
        functools.partial(adagrad_kernel, len(got)),
        [((rows, D), f32), ((1, rows), f32)],
        (own, *got, embed, accum.reshape(1, rows)),
    )
    return new_embed, new_accum.reshape(rows)


def swap(x, axis, size, flip):
    return lax.ppermute(x, axis, [(i, i ^ flip) for i in range(size)])


def hop(x, zero, one):
    pairs = []
    for r in range(8):
        for c in range(32):
            if c % 2 == 0:
                pairs.append((r * 32 + c, r * 32 + (c ^ zero)))
            elif one:
                pairs.append((r * 32 + c, (r ^ one) * 32 + c))
    return lax.ppermute(x, ("row", "col"), pairs)


def per_device(counts, row_marg, col_marg, log_total, row_emb, row_accum, col_emb, col_accum):
    col_swap = lambda x, flip: swap(x, "col", 32, flip)
    row_swap = lambda x, flip: swap(x, "row", 8, flip)
    block = lambda n, t=bf16: ((n, D), t)
    hbm = pl.BlockSpec(memory_space=pltpu.HBM)

    keep = lambda x: pltpu.with_memory_space_constraint(x, pltpu.HBM)
    row, col, out = call(
        first_kernel, [block(64), block(128), block(128)], (keep(row_emb), keep(col_emb)), in_specs=[hbm, hbm],
        scratch=[pltpu.VMEM((64, D), f32), pltpu.VMEM((128, D), f32), pltpu.SemaphoreType.DMA((2,))],
    )
    margs = log_total, row_marg, col_marg, counts
    a, b = call(second_kernel, [block(128)] * 2, (row, col, col_swap(out, 1)))
    near = [hop(a, 2, 1), hop(b, 4, 1), hop(a, 6, 0)]
    weight_a, base_a, token = slope_parts(0, *margs, after=(a,))
    mine = list(call(third_kernel, [block(512)], (token, a, b, *near)))
    mine = mine + [hop(mine[0], 8 * k, 2 * k) for k in (2, 1, 3)]
    weight_b, base_b, token = slope_parts(1, *margs, after=(mine[0],))
    mine = mine[0:1] + [tie(x, token) for x in mine[1:]]
    got = [col_swap(x, 1) for x in mine]

    row_own, row_other, col_own, *col_send = call(
        main_kernel,
        [block(1024, f32), block(1024), block(256, f32)] + [block(256)] * 3,
        (weight_a, base_a, weight_b, base_b, *mine, *got),
        scratch=[pltpu.VMEM((2048, D), bf16), pltpu.VMEM((1024, D), bf16),
                 pltpu.VMEM((2048, D), f32), pltpu.VMEM((1024, D), f32)],
        limit=24,
        cost=pl.CostEstimate(flops=3 << 30, bytes_accessed=16 << 20, transcendentals=2 << 20),
    )

    row_got = col_swap(row_other, 1)
    col_got = [row_swap(col_send[k - 1], 2 * k) for k in (2, 1, 3)]
    row_own, *row_send = fold(row_own, [row_got], 256, 256, 256, 256)
    row_got = [col_swap(row_send[k - 1], 8 * k) for k in (2, 1, 3)]
    col_own, col_last = fold(col_own, col_got, 128, 128)
    col_got = [row_swap(col_last, 1)]
    row_own, *row_send = fold(row_own, row_got, 64, 64, 64, 64)
    row_got = [col_swap(row_send[k - 1], 2 * k) for k in (2, 3, 1)]
    new_col_emb, new_col_accum = adagrad(col_own, col_got, col_emb, col_accum)
    new_row_emb, new_row_accum = adagrad(row_own, row_got, row_emb, row_accum)
    return (new_row_emb, new_row_accum, new_col_emb, new_col_accum)


def solution(mesh):
    return jax.shard_map(
        per_device,
        mesh=mesh,
        in_specs=(
            P("row", "col"),
            P("row"),
            P("col"),
            P(),
            P(("row", "col"), None),
            P(("row", "col")),
            P(("col", "row"), None),
            P(("col", "row")),
        ),
        out_specs=(
            P(("row", "col"), None),
            P(("row", "col")),
            P(("col", "row"), None),
            P(("col", "row")),
        ),
        check_vma=False,
    )
```

```python
import functools
import jax
import jax.numpy as jnp
from jax import lax
from jax.experimental import pallas as pl
from jax.experimental.pallas import tpu as pltpu
from jax.sharding import PartitionSpec as P

learn_rate = 0.5
FIRST = 6
D = 256
f32, bf16 = jnp.float32, jnp.bfloat16
VM = pl.BlockSpec(memory_space=pltpu.VMEM)
SM = pl.BlockSpec(memory_space=pltpu.SMEM)


def call(kernel, outs, ins, in_specs=None, scratch=(), limit=8, cost=None):
    return pl.pallas_call(
        kernel,
        in_specs=in_specs or [VM] * len(ins),
        out_specs=[VM] * len(outs),
        out_shape=[jax.ShapeDtypeStruct(s, t) for s, t in outs],
        scratch_shapes=list(scratch),
        compiler_params=pltpu.CompilerParams(vmem_limit_bytes=limit << 20),
        cost_estimate=cost,
    )(*ins)


def by_core(zero, one):
    core = lax.axis_index("col") % 2
    pl.when(core == 0)(zero)
    pl.when(core == 1)(one)


def first_kernel(row_emb, col_emb, row, col, out, row_buf, col_buf, sem):
    copies = [
        pltpu.make_async_copy(row_emb, row_buf, sem.at[0]),
        pltpu.make_async_copy(col_emb, col_buf, sem.at[1]),
    ]
    for copy in copies:
        copy.start()
    for copy in copies:
        copy.wait()
    row[...] = row_buf[...].astype(bf16)
    col[...] = col_buf[...].astype(bf16)

    def zero():
        out[...] = col_buf[...].astype(bf16)

    def one():
        out[0:64, :] = row_buf[...].astype(bf16)
        out[64:128, :] = jnp.zeros((64, D), bf16)

    by_core(zero, one)


def second_kernel(row, col, got, a, b):
    def zero():
        for out in (a, b):
            out[0:64, :] = row[...]
            out[64:128, :] = got[0:64, :]

    def one():
        a[...] = got[...]
        b[...] = col[...]

    by_core(zero, one)


def third_kernel(token, a, b, g1, g2, g3, out):
    def put(*parts):
        for i, part in enumerate(parts):
            out[i * 128:(i + 1) * 128, :] = part[...]

    by_core(lambda: put(a, g1, g2, g3), lambda: put(a, b, g3, g2))


def tie_kernel(x, *refs):
    refs[-1][...] = x[...]


def tie(x, *after):
    return call(tie_kernel, [(x.shape, x.dtype)], (x, *after))[0]


def slope_parts_kernel(low, groups, after, log_total, row_marg, col_marg, counts, *refs):
    weight, base, token, buf, row_buf, col_buf, sem, row_log, row_half, col_half = refs[after:]
    token[...] = jnp.zeros_like(token)
    me = lax.axis_index("row"), lax.axis_index("col")
    group = lambda i: (me[1] // 2) ^ (i + low)

    def copy(i):
        at = pl.multiple_of(group(i) * 128, 128)
        return pltpu.make_async_copy(counts.at[pl.ds(at, 128), :], buf.at[i], sem.at[i])

    small = [
        pltpu.make_async_copy(row_marg, row_buf, sem.at[groups]),
        pltpu.make_async_copy(col_marg, col_buf, sem.at[groups + 1]),
    ]
    for one in small:
        one.start()
    for i in range(groups):
        copy(i).start()
    row_log[...] = jnp.zeros_like(row_log)
    for one in small:
        one.wait()
    for i in range(groups):
        row_log[i:i + 1, :] = jnp.log(row_buf[pl.ds(group(i), 1), :].astype(f32))
    turned = 0.5 * row_log[...].T
    for i in range(groups):
        row_half[i] = jnp.broadcast_to(turned[:, i:i + 1], (128, 128))
    col_half[...] = 0.5 * (jnp.log(col_buf[...].astype(f32)) - log_total[0])

    def body(i, carry):
        copy(i).wait()
        rows = pl.ds(pl.multiple_of(i * 128, 128), 128)
        shift = row_half[i]
        for j in range(8):
            strip = me[0] ^ j
            n = buf[i, :, pl.ds(pl.multiple_of(strip * 128, 128), 128)].astype(f32)
            present = n > 0.0
            n = jnp.maximum(n, 1.0)
            at = slice(j * 128, (j + 1) * 128)
            weight[rows, at] = jnp.where(present, 0.2 + (0.5 * n) * lax.rsqrt(n), 0.0)
            base[rows, at] = (shift + col_half[pl.ds(strip, 1), :]) - 0.5 * jnp.log(n)
        return carry

    lax.fori_loop(0, groups, body, 0)


def slope_parts(low, groups, log_total, row_marg, col_marg, counts, after=()):
    hbm = pl.BlockSpec(memory_space=pltpu.HBM)
    keep = lambda x: pltpu.with_memory_space_constraint(x, pltpu.HBM)
    return call(
        functools.partial(slope_parts_kernel, low, groups, len(after)),
        [((128 * groups, 1024), f32)] * 2 + [((8, 128), f32)],
        (log_total, keep(row_marg.reshape(16, 128)), keep(col_marg.reshape(8, 128)), keep(counts), *after),
        in_specs=[SM, hbm, hbm, hbm] + [VM] * len(after),
        scratch=[
            pltpu.VMEM((groups, 128, 1024), jnp.int32),
            pltpu.VMEM((16, 128), jnp.int32),
            pltpu.VMEM((8, 128), jnp.int32),
            pltpu.SemaphoreType.DMA((groups + 2,)),
            pltpu.VMEM((128, 128), f32),
            pltpu.VMEM((groups, 128, 128), f32),
            pltpu.VMEM((8, 128), f32),
        ],
        limit=10,
        cost=pl.CostEstimate(flops=0, bytes_accessed=groups * 5 << 18, transcendentals=groups << 18),
    )


def main_kernel(weight_a, base_a, weight_b, base_b, *refs):
    (mine, got, (row_own, row_other, col_own, col_1, col_2, col_3),
     (rows, cols, row_acc, col_acc)) = refs[0:4], refs[4:8], refs[8:14], refs[14:]

    def gather(row_parts, col_parts, core):
        for i, part in zip((0,) + (2, 1, 3), row_parts):
            rows[i * 512:(i + 1) * 512, :] = part[...]
        for i, part in zip((0,) + (2, 1, 3), col_parts):
            for j in range(2):
                at = j * 256 + core * 128
                to = i * 256 + j * 128
                cols[to:to + 128, :] = part[at:at + 128, :]

    by_core(lambda: gather(mine, got, 0), lambda: gather(got, mine, 1))
    for j in range(4):
        at = slice(j * 256, (j + 1) * 256)
        c = cols[at, :]
        col = None
        for h, (weight, base) in enumerate(((weight_a, base_a), (weight_b, base_b))):
            here = slice(FIRST * 128 * h, FIRST * 128 + (2048 - FIRST * 128) * h)
            r = rows[here, :]
            x = lax.dot_general(r * bf16(0.5), c, (((1,), (1,)), ((), ())), preferred_element_type=f32) + base[:, at]
            w = weight[:, at]
            slopes = jnp.where(w > 0.0, w * x, 0.5 * jnp.tanh(x) + 0.5).astype(bf16)
            part = jnp.dot(slopes, c, preferred_element_type=f32)
            row_acc[here, :] = part if j == 0 else row_acc[here, :] + part
            part = lax.dot_general(slopes, r, (((0,), (0,)), ((), ())), preferred_element_type=f32)
            col = part if col is None else col + part
        (col_own, col_1, col_2, col_3)[j][...] = col.astype(f32 if j == 0 else bf16)
    core = lax.axis_index("col") % 2
    for i in range(16):
        to = slice(i * 64, (i + 1) * 64)
        row_own[to, :] = row_acc[pl.ds(pl.multiple_of(i * 128 + core * 64, 64), 64), :]
        row_other[to, :] = row_acc[pl.ds(pl.multiple_of(i * 128 + (1 - core) * 64, 64), 64), :].astype(bf16)


def fold_kernel(n, *refs):
    own, got, outs = refs[0], refs[1:1 + n], refs[1 + n:]
    at = 0
    for out in outs:
        rows = slice(at, at + out.shape[0])
        at += out.shape[0]
        total = own[rows, :]
        for ref in got:
            total = total + ref[rows, :].astype(f32)
        out[...] = total.astype(out.dtype)


def fold(own, got, *parts):
    outs = [((rows, D), bf16 if i else f32) for i, rows in enumerate(parts)]
    return call(functools.partial(fold_kernel, len(got)), outs, (own, *got))


def adagrad_part(grad, embed, accum, embed_out, accum_out):
    rows = embed.shape[0]
    line = jnp.concatenate([accum[...]] * (128 // rows), axis=1)
    column = jnp.broadcast_to(line, (128, 128)).T[0:rows, 0:1]
    new = column + jnp.mean(grad * grad, axis=1, keepdims=True)
    embed_out[...] = embed[...] - learn_rate * grad / jnp.sqrt(new)
    tall = jnp.concatenate([jnp.broadcast_to(new, (rows, 128))] * (128 // rows), axis=0)
    accum_out[...] = tall.T[0:1, 0:rows]


def adagrad_kernel(n, *refs):
    own, got, embed, accum, embed_out, accum_out = refs[0], refs[1:1 + n], *refs[1 + n:]
    grad = own[...]
    for ref in got:
        grad = grad + ref[...].astype(f32)
    adagrad_part(grad, embed, accum, embed_out, accum_out)


def adagrad(own, got, embed, accum):
    rows = own.shape[0]
    new_embed, new_accum = call(
        functools.partial(adagrad_kernel, len(got)),
        [((rows, D), f32), ((1, rows), f32)],
        (own, *got, embed, accum.reshape(1, rows)),
    )
    return new_embed, new_accum.reshape(rows)


def swap(x, axis, size, flip):
    return lax.ppermute(x, axis, [(i, i ^ flip) for i in range(size)])


def hop(x, zero, one):
    pairs = []
    for r in range(8):
        for c in range(32):
            if c % 2 == 0:
                pairs.append((r * 32 + c, r * 32 + (c ^ zero)))
            elif one:
                pairs.append((r * 32 + c, (r ^ one) * 32 + c))
    return lax.ppermute(x, ("row", "col"), pairs)


def per_device(counts, row_marg, col_marg, log_total, row_emb, row_accum, col_emb, col_accum):
    col_swap = lambda x, flip: swap(x, "col", 32, flip)
    row_swap = lambda x, flip: swap(x, "row", 8, flip)
    block = lambda n, t=bf16: ((n, D), t)
    hbm = pl.BlockSpec(memory_space=pltpu.HBM)

    keep = lambda x: pltpu.with_memory_space_constraint(x, pltpu.HBM)
    row, col, out = call(
        first_kernel, [block(64), block(128), block(128)], (keep(row_emb), keep(col_emb)), in_specs=[hbm, hbm],
        scratch=[pltpu.VMEM((64, D), f32), pltpu.VMEM((128, D), f32), pltpu.SemaphoreType.DMA((2,))],
    )
    margs = log_total, row_marg, col_marg, counts
    a, b = call(second_kernel, [block(128)] * 2, (row, col, col_swap(out, 1)))
    near = [hop(a, 2, 0), hop(b, 4, 1), hop(a, 6, 1)]
    weight_a, base_a, token = slope_parts(0, FIRST, *margs, after=(a,))
    mine = list(call(third_kernel, [block(512)], (token, a, b, *near)))
    mine = mine + [hop(mine[0], 8 * k, 2 * k) for k in (2, 1, 3)]
    weight_b, base_b, token = slope_parts(FIRST, 16 - FIRST, *margs, after=(mine[0],))
    mine = mine[0:1] + [tie(x, token) for x in mine[1:]]
    got = [col_swap(x, 1) for x in mine]

    row_own, row_other, col_own, *col_send = call(
        main_kernel,
        [block(1024, f32), block(1024), block(256, f32)] + [block(256)] * 3,
        (weight_a, base_a, weight_b, base_b, *mine, *got),
        scratch=[pltpu.VMEM((2048, D), bf16), pltpu.VMEM((1024, D), bf16),
                 pltpu.VMEM((2048, D), f32), pltpu.VMEM((1024, D), f32)],
        limit=24,
        cost=pl.CostEstimate(flops=3 << 30, bytes_accessed=16 << 20, transcendentals=2 << 20),
    )

    row_got = col_swap(row_other, 1)
    col_got = [row_swap(col_send[k - 1], 2 * k) for k in (2, 1, 3)]
    row_own, *row_send = fold(row_own, [row_got], 256, 256, 256, 256)
    row_got = [col_swap(row_send[k - 1], 8 * k) for k in (2, 1, 3)]
    col_own, col_last = fold(col_own, col_got, 128, 128)
    col_got = [row_swap(col_last, 1)]
    row_own, *row_send = fold(row_own, row_got, 64, 64, 64, 64)
    row_got = [col_swap(row_send[k - 1], 2 * k) for k in (2, 3, 1)]
    new_col_emb, new_col_accum = adagrad(col_own, col_got, col_emb, col_accum)
    new_row_emb, new_row_accum = adagrad(row_own, row_got, row_emb, row_accum)
    return (new_row_emb, new_row_accum, new_col_emb, new_col_accum)


def solution(mesh):
    return jax.shard_map(
        per_device,
        mesh=mesh,
        in_specs=(
            P("row", "col"),
            P("row"),
            P("col"),
            P(),
            P(("row", "col"), None),
            P(("row", "col")),
            P(("col", "row"), None),
            P(("col", "row")),
        ),
        out_specs=(
            P(("row", "col"), None),
            P(("row", "col")),
            P(("col", "row"), None),
            P(("col", "row")),
        ),
        check_vma=False,
    )
```

```python
import functools
import jax
import jax.numpy as jnp
from jax import lax
from jax.experimental import pallas as pl
from jax.experimental.pallas import tpu as pltpu
from jax.sharding import PartitionSpec as P

learn_rate = 0.5
FIRST = 6
D = 256
f32, bf16 = jnp.float32, jnp.bfloat16
VM = pl.BlockSpec(memory_space=pltpu.VMEM)
SM = pl.BlockSpec(memory_space=pltpu.SMEM)


def call(kernel, outs, ins, in_specs=None, scratch=(), limit=8, cost=None):
    return pl.pallas_call(
        kernel,
        in_specs=in_specs or [VM] * len(ins),
        out_specs=[VM] * len(outs),
        out_shape=[jax.ShapeDtypeStruct(s, t) for s, t in outs],
        scratch_shapes=list(scratch),
        compiler_params=pltpu.CompilerParams(vmem_limit_bytes=limit << 20),
        cost_estimate=cost,
    )(*ins)


def by_core(zero, one):
    core = lax.axis_index("col") % 2
    pl.when(core == 0)(zero)
    pl.when(core == 1)(one)


def first_kernel(row_emb, col_emb, row, col, out, row_buf, col_buf, sem):
    copies = [
        pltpu.make_async_copy(row_emb, row_buf, sem.at[0]),
        pltpu.make_async_copy(col_emb, col_buf, sem.at[1]),
    ]
    for copy in copies:
        copy.start()
    for copy in copies:
        copy.wait()
    row[...] = row_buf[...].astype(bf16)
    col[...] = col_buf[...].astype(bf16)

    def zero():
        out[...] = col_buf[...].astype(bf16)

    def one():
        out[0:64, :] = row_buf[...].astype(bf16)
        out[64:128, :] = jnp.zeros((64, D), bf16)

    by_core(zero, one)


def second_kernel(row, col, got, a, b):
    def zero():
        for out in (a, b):
            out[0:64, :] = row[...]
            out[64:128, :] = got[0:64, :]

    def one():
        a[...] = got[...]
        b[...] = col[...]

    by_core(zero, one)


def third_kernel(token, a, b, g1, g2, g3, out):
    def put(*parts):
        for i, part in enumerate(parts):
            out[i * 128:(i + 1) * 128, :] = part[...]

    by_core(lambda: put(a, g1, g2, g3), lambda: put(a, b, g3, g2))


def tie_kernel(x, *refs):
    refs[-1][...] = x[...]


def tie(x, *after):
    return call(tie_kernel, [(x.shape, x.dtype)], (x, *after))[0]


def slope_parts_kernel(low, groups, after, log_total, row_marg, col_marg, counts, *refs):
    weight, base, token, buf, row_buf, col_buf, sem, row_log, row_half, col_half = refs[after:]
    token[...] = jnp.zeros_like(token)
    me = lax.axis_index("row"), lax.axis_index("col")
    group = lambda i: (me[1] // 2) ^ (i + low)

    def copy(i):
        at = pl.multiple_of(group(i) * 128, 128)
        return pltpu.make_async_copy(counts.at[pl.ds(at, 128), :], buf.at[i], sem.at[i])

    small = [
        pltpu.make_async_copy(row_marg, row_buf, sem.at[groups]),
        pltpu.make_async_copy(col_marg, col_buf, sem.at[groups + 1]),
    ]
    for one in small:
        one.start()
    for i in range(groups):
        copy(i).start()
    row_log[...] = jnp.zeros_like(row_log)
    for one in small:
        one.wait()
    for i in range(groups):
        row_log[i:i + 1, :] = jnp.log(row_buf[pl.ds(group(i), 1), :].astype(f32))
    turned = 0.5 * row_log[...].T
    for i in range(groups):
        row_half[i] = jnp.broadcast_to(turned[:, i:i + 1], (128, 128))
    col_half[...] = 0.5 * (jnp.log(col_buf[...].astype(f32)) - log_total[0])

    def body(i, carry):
        copy(i).wait()
        rows = pl.ds(pl.multiple_of(i * 128, 128), 128)
        shift = row_half[i]
        for j in range(8):
            strip = me[0] ^ j
            n = buf[i, :, pl.ds(pl.multiple_of(strip * 128, 128), 128)].astype(f32)
            present = n > 0.0
            n = jnp.maximum(n, 1.0)
            at = slice(j * 128, (j + 1) * 128)
            weight[rows, at] = jnp.where(present, 0.2 + (0.5 * n) * lax.rsqrt(n), 0.0)
            base[rows, at] = (shift + col_half[pl.ds(strip, 1), :]) - 0.5 * jnp.log(n)
        return carry

    lax.fori_loop(0, groups, body, 0)


def slope_parts(low, groups, log_total, row_marg, col_marg, counts, after=()):
    hbm = pl.BlockSpec(memory_space=pltpu.HBM)
    keep = lambda x: pltpu.with_memory_space_constraint(x, pltpu.HBM)
    return call(
        functools.partial(slope_parts_kernel, low, groups, len(after)),
        [((128 * groups, 1024), f32)] * 2 + [((8, 128), f32)],
        (log_total, keep(row_marg.reshape(16, 128)), keep(col_marg.reshape(8, 128)), keep(counts), *after),
        in_specs=[SM, hbm, hbm, hbm] + [VM] * len(after),
        scratch=[
            pltpu.VMEM((groups, 128, 1024), jnp.int32),
            pltpu.VMEM((16, 128), jnp.int32),
            pltpu.VMEM((8, 128), jnp.int32),
            pltpu.SemaphoreType.DMA((groups + 2,)),
            pltpu.VMEM((128, 128), f32),
            pltpu.VMEM((groups, 128, 128), f32),
            pltpu.VMEM((8, 128), f32),
        ],
        limit=10,
        cost=pl.CostEstimate(flops=0, bytes_accessed=groups * 5 << 18, transcendentals=groups << 18),
    )


def main_kernel(weight_a, base_a, weight_b, base_b, *refs):
    (mine, got, (row_own, row_other, col_own, col_1, col_2, col_3),
     (rows, cols, row_acc, col_acc)) = refs[0:4], refs[4:8], refs[8:14], refs[14:]

    def gather(row_parts, col_parts, core):
        for i, part in zip((0,) + (2, 1, 3), row_parts):
            rows[i * 512:(i + 1) * 512, :] = part[...]
        for i, part in zip((0,) + (2, 1, 3), col_parts):
            for j in range(2):
                at = j * 256 + core * 128
                to = i * 256 + j * 128
                cols[to:to + 128, :] = part[at:at + 128, :]

    by_core(lambda: gather(mine, got, 0), lambda: gather(got, mine, 1))
    for j in range(4):
        at = slice(j * 256, (j + 1) * 256)
        c = cols[at, :]
        col = None
        for h, (weight, base) in enumerate(((weight_a, base_a), (weight_b, base_b))):
            here = slice(FIRST * 128 * h, FIRST * 128 + (2048 - FIRST * 128) * h)
            r = rows[here, :]
            x = lax.dot_general(r * bf16(0.5), c, (((1,), (1,)), ((), ())), preferred_element_type=f32) + base[:, at]
            w = weight[:, at]
            slopes = jnp.where(w > 0.0, w * x, 0.5 * jnp.tanh(x) + 0.5).astype(bf16)
            part = jnp.dot(slopes, c, preferred_element_type=f32)
            row_acc[here, :] = part if j == 0 else row_acc[here, :] + part
            part = lax.dot_general(slopes, r, (((0,), (0,)), ((), ())), preferred_element_type=f32)
            col = part if col is None else col + part
        (col_own, col_1, col_2, col_3)[j][...] = col.astype(f32 if j == 0 else bf16)
    core = lax.axis_index("col") % 2
    for i in range(16):
        to = slice(i * 64, (i + 1) * 64)
        row_own[to, :] = row_acc[pl.ds(pl.multiple_of(i * 128 + core * 64, 64), 64), :]
        row_other[to, :] = row_acc[pl.ds(pl.multiple_of(i * 128 + (1 - core) * 64, 64), 64), :].astype(bf16)


def fold_kernel(n, *refs):
    own, got, outs = refs[0], refs[1:1 + n], refs[1 + n:]
    at = 0
    for out in outs:
        rows = slice(at, at + out.shape[0])
        at += out.shape[0]
        total = own[rows, :]
        for ref in got:
            total = total + ref[rows, :].astype(f32)
        out[...] = total.astype(out.dtype)


def fold(own, got, *parts):
    outs = [((rows, D), bf16 if i else f32) for i, rows in enumerate(parts)]
    return call(functools.partial(fold_kernel, len(got)), outs, (own, *got))


def adagrad_part(grad, embed, accum, embed_out, accum_out):
    rows = embed.shape[0]
    line = jnp.concatenate([accum[...]] * (128 // rows), axis=1)
    column = jnp.broadcast_to(line, (128, 128)).T[0:rows, 0:1]
    new = column + jnp.mean(grad * grad, axis=1, keepdims=True)
    embed_out[...] = embed[...] - learn_rate * grad / jnp.sqrt(new)
    tall = jnp.concatenate([jnp.broadcast_to(new, (rows, 128))] * (128 // rows), axis=0)
    accum_out[...] = tall.T[0:1, 0:rows]


def adagrad_kernel(n, *refs):
    own, got, embed, accum, embed_out, accum_out = refs[0], refs[1:1 + n], *refs[1 + n:]
    grad = own[...]
    for ref in got:
        grad = grad + ref[...].astype(f32)
    adagrad_part(grad, embed, accum, embed_out, accum_out)


def adagrad(own, got, embed, accum):
    rows = own.shape[0]
    new_embed, new_accum = call(
        functools.partial(adagrad_kernel, len(got)),
        [((rows, D), f32), ((1, rows), f32)],
        (own, *got, embed, accum.reshape(1, rows)),
    )
    return new_embed, new_accum.reshape(rows)


def swap(x, axis, size, flip):
    return lax.ppermute(x, axis, [(i, i ^ flip) for i in range(size)])


def hop(x, zero, one):
    pairs = []
    for r in range(8):
        for c in range(32):
            if c % 2 == 0:
                pairs.append((r * 32 + c, r * 32 + (c ^ zero)))
            elif one:
                pairs.append((r * 32 + c, (r ^ one) * 32 + c))
    return lax.ppermute(x, ("row", "col"), pairs)


def per_device(counts, row_marg, col_marg, log_total, row_emb, row_accum, col_emb, col_accum):
    col_swap = lambda x, flip: swap(x, "col", 32, flip)
    row_swap = lambda x, flip: swap(x, "row", 8, flip)
    block = lambda n, t=bf16: ((n, D), t)
    hbm = pl.BlockSpec(memory_space=pltpu.HBM)

    keep = lambda x: pltpu.with_memory_space_constraint(x, pltpu.HBM)
    row, col, out = call(
        first_kernel, [block(64), block(128), block(128)], (keep(row_emb), keep(col_emb)), in_specs=[hbm, hbm],
        scratch=[pltpu.VMEM((64, D), f32), pltpu.VMEM((128, D), f32), pltpu.SemaphoreType.DMA((2,))],
    )
    margs = log_total, row_marg, col_marg, counts
    a, b = call(second_kernel, [block(128)] * 2, (row, col, col_swap(out, 1)))
    near = [hop(a, 2, 0), hop(b, 4, 1), hop(a, 6, 1)]
    weight_a, base_a, token = slope_parts(0, FIRST, *margs, after=(a,))
    mine = list(call(third_kernel, [block(512)], (token, a, b, *near)))
    mine = mine + [hop(mine[0], 8 * k, 2 * k) for k in (2, 1, 3)]
    weight_b, base_b, token = slope_parts(FIRST, 16 - FIRST, *margs, after=(mine[0],))
    mine = [tie(x, token) for x in mine]
    got = [col_swap(x, 1) for x in mine]

    row_own, row_other, col_own, *col_send = call(
        main_kernel,
        [block(1024, f32), block(1024), block(256, f32)] + [block(256)] * 3,
        (weight_a, base_a, weight_b, base_b, *mine, *got),
        scratch=[pltpu.VMEM((2048, D), bf16), pltpu.VMEM((1024, D), bf16),
                 pltpu.VMEM((2048, D), f32), pltpu.VMEM((1024, D), f32)],
        limit=24,
        cost=pl.CostEstimate(flops=3 << 30, bytes_accessed=16 << 20, transcendentals=2 << 20),
    )

    row_got = col_swap(row_other, 1)
    col_got = [row_swap(col_send[k - 1], 2 * k) for k in (2, 1, 3)]
    row_own, *row_send = fold(row_own, [row_got], 256, 256, 256, 256)
    row_got = [col_swap(row_send[k - 1], 8 * k) for k in (2, 1, 3)]
    col_own, col_last = fold(col_own, col_got, 128, 128)
    col_got = [row_swap(col_last, 1)]
    row_own, *row_send = fold(row_own, row_got, 64, 64, 64, 64)
    row_got = [col_swap(row_send[k - 1], 2 * k) for k in (2, 3, 1)]
    new_col_emb, new_col_accum = adagrad(col_own, col_got, col_emb, col_accum)
    new_row_emb, new_row_accum = adagrad(row_own, row_got, row_emb, row_accum)
    return (new_row_emb, new_row_accum, new_col_emb, new_col_accum)


def solution(mesh):
    return jax.shard_map(
        per_device,
        mesh=mesh,
        in_specs=(
            P("row", "col"),
            P("row"),
            P("col"),
            P(),
            P(("row", "col"), None),
            P(("row", "col")),
            P(("col", "row"), None),
            P(("col", "row")),
        ),
        out_specs=(
            P(("row", "col"), None),
            P(("row", "col")),
            P(("col", "row"), None),
            P(("col", "row")),
        ),
        check_vma=False,
    )
```
